256 devices in a mesh: row: 16 (over z, y_hi), col: 16 (over y_lo, x, core).
Axes of the slice: x: 4, y: 4 (y_hi: 2, y_lo: 2; y = y_hi * 2 + y_lo), z: 8, core: 2. Of those that a mesh axis runs over, the one named last changes fastest.
Arguments:
- tokens: bfloat16 [1024, 12288], P('col', 'row'), may hold values from -6 to 6
- out_grad: bfloat16 [1024, 12288], P('col', 'row'), may hold values from -1.5 to 1.5
- w_in: bfloat16 [12288, 24576], P('row', 'col'), may hold values from -0.0546875 to 0.0546875
- b_in: float32 [24576], P('col'), may hold values from -3 to 3
- w_out: bfloat16 [24576, 12288], P('col', 'row'), may hold values from -0.0390625 to 0.0390625
Outputs:
- grad_tokens: bfloat16 [1024, 12288], P('col', 'row')
- grad_w_in: bfloat16 [12288, 24576], P('row', 'col')
- grad_b_in: float32 [24576], P(('col', 'row'))
- grad_w_out: bfloat16 [24576, 12288], P('col', 'row')
The draws below stay inside these ranges and needn't reach their ends.
All inputs are finite; a program needn't handle non-finite values.
Results may differ from the reference program's by a relative error of at most 0.0049.
Values may be sent and summed in bfloat16 or wider, within the bound.
No kernel may reach another device: no remote copies, remote signals or barrier semaphores. Data moves between devices by JAX's collectives and lax.ppermute only.
A program may use at most 128 MiB of HBM per device.

```python
import jax
import jax.numpy as jnp
from jax import lax

D = 12288
FF = 24576
TOKENS = 1024


def block_scale(stream_key, dims, split, smallest, high):
    def one(dim, blocks):
        heights = jax.random.uniform(jax.random.fold_in(jax.random.fold_in(stream_key, 6), dim), (blocks,), jnp.float32, smallest / len(split), high / len(split))
        return jnp.repeat(jnp.exp(heights), dims[dim] // blocks).reshape((-1,) + (1,) * (len(dims) - dim - 1))

    loudness = one(*split[0])
    for cut in split[1:]:
        loudness = loudness * one(*cut)
    return loudness


def scatter_about(key, dims, deviation, most, shards=(), held_as=jnp.bfloat16):
    drawn = jax.random.normal(key, dims, jnp.float32) * deviation
    if len(shards) > 0:
        drawn = block_scale(key, dims, shards, -0.22, 0.18) * drawn
    return jnp.clip(drawn, min=-most, max=most).astype(held_as)


def setup_inputs(seed: int = 0) -> dict:
    key_of = jax.random.split(jax.random.key(seed), 6)
    tokens = scatter_about(key_of[0], (TOKENS, D), 1.0, 6.0, ((0, 16), (1, 16)))
    out_grad = scatter_about(key_of[1], (TOKENS, D), 0.25, 1.5, ((0, 16), (1, 16)))
    w_in = scatter_about(key_of[2], (D, FF), D ** -0.5, 0.0546875, ((0, 16), (1, 16)))
    b_in = scatter_about(key_of[3], (FF,), 0.5, 3.0, ((0, 16),), jnp.float32)
    w_out = scatter_about(key_of[4], (FF, D), FF ** -0.5, 0.0390625, ((0, 16), (1, 16)))
    return dict(tokens=tokens, out_grad=out_grad, w_in=w_in, b_in=b_in, w_out=w_out)


gelu_scale = 0.7978845608
cubic = 0.044715


def gelu_pair(value):
    inner = jnp.tanh(gelu_scale * (value + cubic * value * value * value))
    output = 0.5 * value * (1.0 + inner)
    slope = 0.5 * (1.0 + inner) + 0.5 * value * (1.0 - inner * inner) * gelu_scale * (1.0 + 3.0 * cubic * value * value)
    return output, slope


def reference(tokens, out_grad, w_in, b_in, w_out):
    pre_act = jnp.dot(tokens, w_in, preferred_element_type=jnp.float32) + b_in
    back_grad = lax.dot_general(out_grad, w_out, (((1,), (1,)), ((), ())), preferred_element_type=jnp.float32)
    output, slope = gelu_pair(pre_act)
    activation = output.astype(jnp.bfloat16)
    hidden_grad = (back_grad * slope).astype(jnp.bfloat16)
    grad_tokens = lax.dot_general(hidden_grad, w_in, (((1,), (1,)), ((), ())), preferred_element_type=jnp.float32).astype(jnp.bfloat16)
    grad_w_in = lax.dot_general(tokens, hidden_grad, (((0,), (0,)), ((), ())), preferred_element_type=jnp.float32).astype(jnp.bfloat16)
    grad_b_in = jnp.sum(hidden_grad.astype(jnp.float32), axis=0)
    grad_w_out = lax.dot_general(activation, out_grad, (((0,), (0,)), ((), ())), preferred_element_type=jnp.float32).astype(jnp.bfloat16)
    return (grad_tokens, grad_w_in, grad_b_in, grad_w_out)
```

```python
import jax
import jax.numpy as jnp
from jax import lax
from jax.sharding import PartitionSpec as P

gelu_scale = 0.7978845608
cubic = 0.044715
Z, YH, YL, X, CORES = 8, 2, 2, 4, 2
CHIPS = YL * X


def gelu_pair(value):
    inner = jnp.tanh(gelu_scale * (value + cubic * value * value * value))
    output = 0.5 * value * (1.0 + inner)
    slope = 0.5 * (1.0 + inner) + 0.5 * value * (1.0 - inner * inner) * gelu_scale * (
        1.0 + 3.0 * cubic * value * value
    )
    return (output, slope)


def dot(left, right, left_dim, right_dim):
    return lax.dot_general(
        left, right, (((left_dim,), (right_dim,)), ((), ())), preferred_element_type=jnp.float32
    )


def number(z, yh, yl, x, core):
    return (z * YH + yh) * (CHIPS * CORES) + (yl * X + x) * CORES + core


def places():
    for z in range(Z):
        for yh in range(YH):
            for yl in range(YL):
                for x in range(X):
                    for core in range(CORES):
                        yield z, yh, yl, x, core


def permute(value, target):
    pairs = [(number(*place), number(*target(*place))) for place in places()]
    return lax.ppermute(value, ("row", "col"), pairs)


def along_z(value, step):
    return permute(value, lambda z, yh, yl, x, core: ((z + step) % Z, yh, yl, x, core))


def across_yh(value):
    return permute(value, lambda z, yh, yl, x, core: (z, 1 - yh, yl, x, core))


def across_core(value):
    return permute(value, lambda z, yh, yl, x, core: (z, yh, yl, x, 1 - core))


def chip_of(z, yl, x, turn):
    other = (z + turn) % CHIPS
    return yl ^ (other // X), (x + other % X) % X


def chip_from(z, yl, x, turn):
    other = (z + turn) % CHIPS
    return yl ^ (other // X), (x - other % X) % X


def fetch_chip(value, turn):
    def target(z, yh, yl, x, core):
        to_yl, to_x = chip_from(z, yl, x, turn)
        return z, yh, to_yl, to_x, core

    return permute(value, target)


def give_chip(value, turn):
    def target(z, yh, yl, x, core):
        to_yl, to_x = chip_of(z, yl, x, turn)
        return z, yh, to_yl, to_x, core

    return permute(value, target)


def biggest(value):
    return jnp.max(jnp.abs(value)).astype(jnp.float32)


def per_device(tokens, out_grad, w_in, b_in, w_out):
    width, units = w_in.shape
    bounds = lax.pmax(
        jnp.stack([biggest(tokens), biggest(w_in), biggest(out_grad), biggest(w_out)]),
        ("row", "col"),
    )
    whole = width * Z * YH
    pre_scale = 32768.0 / jnp.maximum(whole * bounds[0] * bounds[1], 1e-33)
    back_scale = 32768.0 / jnp.maximum(whole * bounds[2] * bounds[3], 1e-33)

    own = jnp.concatenate([tokens, out_grad], axis=1)
    order = (4, 3, 5, 2, 6, 1, 7, 0)
    near = {turn: fetch_chip(own, turn) for turn in order}
    blocks = {}
    for group in (order[:3], order[3:]):
        mine = jnp.concatenate([near[turn] for turn in group], axis=0)
        theirs = across_core(mine)
        rows = own.shape[0]
        for place, turn in enumerate(group):
            blocks[turn] = jnp.concatenate(
                [near[turn], theirs[place * rows : (place + 1) * rows]], axis=0
            )

    def pre_part(turn):
        return dot(blocks[turn][:, :width], w_in, 1, 0) * pre_scale

    def back_part(turn):
        return dot(blocks[turn][:, width:], w_out, 1, 1) * back_scale

    def ring_sum(part, first):
        moved = along_z(part(4).astype(jnp.float16), first).astype(jnp.float32)
        far, close = part(4 - first) + moved, part(4 + first)
        for left in (2, 1, 0):
            far = along_z(far.astype(jnp.float16), first).astype(jnp.float32)
            close = along_z(close.astype(jnp.float16), -first).astype(jnp.float32)
            if left:
                far = far + part(left * first % Z)
                close = close + part(-left * first % Z)
        return far + close + part(0)

    def both_yh(total):
        sent = total.astype(jnp.float16)
        return sent.astype(jnp.float32) + across_yh(sent).astype(jnp.float32)

    pre_act = both_yh(ring_sum(pre_part, 1)) / pre_scale + b_in
    back = both_yh(ring_sum(back_part, -1)) / back_scale
    output, slope = gelu_pair(pre_act)
    activation = output.astype(jnp.bfloat16)
    hidden = (back * slope).astype(jnp.bfloat16)

    def ring_gather(value, first):
        got = {0: value}
        up, down = value, value
        for step in (1, 2, 3):
            up, down = along_z(up, 1), along_z(down, -1)
            got[-step % Z], got[step] = up, down
        got[4] = along_z(up if first == 1 else down, first)
        return jnp.concatenate([got[turn] for turn in range(Z)], axis=0)

    act_all = ring_gather(activation, 1)
    hid_all = ring_gather(hidden, -1)
    panel = jnp.concatenate([blocks[turn] for turn in range(Z)], axis=0)

    gw_out = dot(act_all, panel[:, width:], 0, 0).astype(jnp.bfloat16)
    gw_in = dot(panel[:, :width], hid_all, 0, 0).astype(jnp.bfloat16)
    grad_part = dot(hid_all, w_in, 1, 1).reshape(Z, CORES, tokens.shape[0], width)
    theirs = across_core(grad_part[:, 1].astype(jnp.bfloat16))
    grad_sum = (grad_part[:, 0] + theirs).astype(jnp.bfloat16)
    grad_tokens = 0.0
    for turn in range(Z):
        grad_tokens = grad_tokens + give_chip(grad_sum[turn], turn).astype(jnp.float32)
    share = units // (Z * YH)
    own_units = lax.dynamic_slice_in_dim(hid_all, lax.axis_index("row") * share, share, 1)
    bias = jnp.sum(own_units.astype(jnp.float32), axis=0)
    return grad_tokens.astype(jnp.bfloat16), gw_in, bias, gw_out


def solution(mesh):
    in_specs = (P("col", "row"), P("col", "row"), P("row", "col"), P("col"), P("col", "row"))
    out_specs = (P("col", "row"), P("row", "col"), P(("col", "row")), P("col", "row"))
    return jax.shard_map(
        per_device, mesh=mesh, in_specs=in_specs, out_specs=out_specs, check_vma=False
    )
```

```python
import jax
import jax.numpy as jnp
from jax import lax
from jax.sharding import PartitionSpec as P

gelu_scale = 0.7978845608
cubic = 0.044715
Z, YH, YL, X, CORES = 8, 2, 2, 4, 2
CHIPS = YL * X


def gelu_pair(value):
    inner = jnp.tanh(gelu_scale * (value + cubic * value * value * value))
    output = 0.5 * value * (1.0 + inner)
    slope = 0.5 * (1.0 + inner) + 0.5 * value * (1.0 - inner * inner) * gelu_scale * (
        1.0 + 3.0 * cubic * value * value
    )
    return (output, slope)


def dot(left, right, left_dim, right_dim):
    return lax.dot_general(
        left, right, (((left_dim,), (right_dim,)), ((), ())), preferred_element_type=jnp.float32
    )


def number(z, yh, yl, x, core):
    return (z * YH + yh) * (CHIPS * CORES) + (yl * X + x) * CORES + core


def places():
    for z in range(Z):
        for yh in range(YH):
            for yl in range(YL):
                for x in range(X):
                    for core in range(CORES):
                        yield z, yh, yl, x, core


def permute(value, target):
    pairs = [(number(*place), number(*target(*place))) for place in places()]
    return lax.ppermute(value, ("row", "col"), pairs)


def along_z(value, step):
    return permute(value, lambda z, yh, yl, x, core: ((z + step) % Z, yh, yl, x, core))


def along_x(value, step):
    return permute(value, lambda z, yh, yl, x, core: (z, yh, yl, (x + step) % X, core))


def across_yh(value):
    return permute(value, lambda z, yh, yl, x, core: (z, 1 - yh, yl, x, core))


def across_yl(value):
    return permute(value, lambda z, yh, yl, x, core: (z, yh, 1 - yl, x, core))


def across_core(value):
    return permute(value, lambda z, yh, yl, x, core: (z, yh, yl, x, 1 - core))


def joined(value):
    return jnp.concatenate([value, across_yl(value)], axis=0)


def spread(pair):
    mine = jnp.concatenate([pair] + [along_x(pair, -d) for d in range(1, X)], axis=0)
    return jnp.concatenate([mine, across_core(mine)], axis=0)


def coded(value, top):
    root = jnp.sqrt(jnp.sqrt(jnp.abs(value) * 2.0 ** (60 - top)))
    return jnp.where(value < 0, -root, root).astype(jnp.float16)


def decoded(code, top):
    root = code.astype(jnp.float32)
    return root * jnp.abs(root) * (root * root) * 2.0 ** (top - 60)


def after(value, *others):
    return lax.optimization_barrier((value,) + others)[0]


HIDDEN_TOP, TOKEN_TOP = 12, 20


def code(value):
    return coded(value, HIDDEN_TOP)


def decode(value):
    return decoded(value, HIDDEN_TOP)


def ring_sum(part, first, begun, gates):
    ends = []
    gate = gates[0] if gates else ()
    moved = along_z(after(code(begun), *gate), first)
    ends.append((moved,))
    far = decode(moved) + part(4 - first)
    close = part(4 + first)
    for left in (2, 1, 0):
        gate = gates[3 - left] if gates else ()
        far = along_z(after(code(far), *gate), first)
        close = along_z(after(code(close), *gate), -first)
        ends.append((far, close))
        far, close = decode(far), decode(close)
        if left:
            far, close = far + part(left * first % Z), close + part(-left * first % Z)
    return code(far + close + part(0)), ends


def both_yh(value):
    return decode(value) + decode(across_yh(value))


def per_device(tokens, out_grad, w_in, b_in, w_out):
    rows, width = tokens.shape
    units = w_in.shape[1]
    shard = rows * CORES
    row_index = lax.axis_index("row")
    z = row_index // YH

    def place(turn):
        return (z + turn) % Z * shard

    def block(whole, turn):
        return lax.dynamic_slice_in_dim(whole, place(turn), shard, 0)

    tok_panel = spread(joined(tokens))
    grad_pair, tok_panel = lax.optimization_barrier((joined(out_grad), tok_panel))
    grad_panel = spread(grad_pair)

    pre_first = dot(block(tok_panel, 4), w_in, 1, 0)
    pre_part = dot(after(tok_panel, pre_first), w_in, 1, 0)
    back_first = dot(block(grad_panel, 4), w_out, 1, 1)
    back_part = dot(after(grad_panel, back_first), w_out, 1, 1)
    pre, ends = ring_sum(lambda turn: block(pre_part, turn), 1, pre_first, ())
    back, _ = ring_sum(lambda turn: block(back_part, turn), -1, back_first, ends)
    output, slope = gelu_pair(both_yh(pre) + b_in)
    activation = output.astype(jnp.bfloat16)
    hidden = (both_yh(back) * slope).astype(jnp.bfloat16)

    def ring_gather(value, first, gates):
        got = {0: value}
        up, down = value, value
        ends = []
        for step in (1, 2, 3):
            gate = gates[step - 1] if gates else ()
            up, down = along_z(after(up, *gate), 1), along_z(after(down, *gate), -1)
            got[-step % Z], got[step] = up, down
            ends.append((up, down))
        got[4] = along_z(up if first == 1 else down, first)
        return got, ends

    def laid(got):
        whole = jnp.zeros((Z * shard, units), jnp.bfloat16)
        for turn in (0, 7, 1, 6, 2, 5, 3, 4):
            whole = lax.dynamic_update_slice_in_dim(whole, got[turn], place(turn), 0)
        return whole

    act, ends = ring_gather(activation, 1, ())
    hid, _ = ring_gather(hidden, -1, ends)
    hid_all = laid(hid)

    half = Z * shard // CORES
    theirs = across_core(coded(dot(hid_all[half:], w_in, 1, 1), TOKEN_TOP))
    mine = dot(hid_all[:half], w_in, 1, 1) + decoded(theirs, TOKEN_TOP)
    sent = coded(mine, TOKEN_TOP)
    total = mine[:shard]
    for d in range(1, X):
        came = along_x(sent[d * shard : (d + 1) * shard], d)
        total = total + decoded(came, TOKEN_TOP)
    last = coded(total[rows:], TOKEN_TOP)
    grad_tokens = total[:rows] + decoded(across_yl(last), TOKEN_TOP)
    grad_tokens = grad_tokens.astype(jnp.bfloat16)

    gw_in = dot(after(tok_panel, sent), hid_all, 0, 0).astype(jnp.bfloat16)
    act[4] = after(act[4], last)
    act_all = laid(act)
    gw_out = dot(act_all, grad_panel, 0, 0).astype(jnp.bfloat16)
    share = units // (Z * YH)
    own_units = lax.dynamic_slice_in_dim(hid_all, row_index * share, share, 1)
    bias = jnp.sum(own_units.astype(jnp.float32), axis=0)
    return grad_tokens, gw_in, bias, gw_out


def solution(mesh):
    in_specs = (P("col", "row"), P("col", "row"), P("row", "col"), P("col"), P("col", "row"))
    out_specs = (P("col", "row"), P("row", "col"), P(("col", "row")), P("col", "row"))
    return jax.shard_map(
        per_device, mesh=mesh, in_specs=in_specs, out_specs=out_specs, check_vma=False
    )
```

```python
import jax
import jax.numpy as jnp
from jax import lax
from jax.sharding import PartitionSpec as P

gelu_scale = 0.7978845608
cubic = 0.044715
Z, YH, YL, X, CORES = 8, 2, 2, 4, 2
CHIPS = YL * X


def gelu_pair(value):
    inner = jnp.tanh(gelu_scale * (value + cubic * value * value * value))
    output = 0.5 * value * (1.0 + inner)
    slope = 0.5 * (1.0 + inner) + 0.5 * value * (1.0 - inner * inner) * gelu_scale * (
        1.0 + 3.0 * cubic * value * value
    )
    return (output, slope)


def dot(left, right, left_dim, right_dim):
    return lax.dot_general(
        left, right, (((left_dim,), (right_dim,)), ((), ())), preferred_element_type=jnp.float32
    )


def number(z, yh, yl, x, core):
    return (z * YH + yh) * (CHIPS * CORES) + (yl * X + x) * CORES + core


def places():
    for z in range(Z):
        for yh in range(YH):
            for yl in range(YL):
                for x in range(X):
                    for core in range(CORES):
                        yield z, yh, yl, x, core


def permute(value, target):
    pairs = [(number(*place), number(*target(*place))) for place in places()]
    return lax.ppermute(value, ("row", "col"), pairs)


def along_z(value, step):
    return permute(value, lambda z, yh, yl, x, core: ((z + step) % Z, yh, yl, x, core))


def along_x(value, step):
    return permute(value, lambda z, yh, yl, x, core: (z, yh, yl, (x + step) % X, core))


def across_yh(value):
    return permute(value, lambda z, yh, yl, x, core: (z, 1 - yh, yl, x, core))


def across_yl(value):
    return permute(value, lambda z, yh, yl, x, core: (z, yh, 1 - yl, x, core))


def across_core(value):
    return permute(value, lambda z, yh, yl, x, core: (z, yh, yl, x, 1 - core))


def joined(value):
    return jnp.concatenate([value, across_yl(value)], axis=0)


def spread(pair):
    mine = jnp.concatenate([pair] + [along_x(pair, -d) for d in range(1, X)], axis=0)
    return jnp.concatenate([mine, across_core(mine)], axis=0)


def coded(value, top):
    root = jnp.sqrt(jnp.sqrt(jnp.abs(value) * 2.0 ** (60 - top)))
    return jnp.where(value < 0, -root, root).astype(jnp.float16)


def decoded(code, top):
    root = code.astype(jnp.float32)
    return root * jnp.abs(root) * (root * root) * 2.0 ** (top - 60)


def after(value, *others):
    return lax.optimization_barrier((value,) + others)[0]


def once(value, other):
    edge = other[:1, : value.shape[1]]
    return jnp.where(edge != edge, jnp.zeros_like(value), value)


HIDDEN_TOP, TOKEN_TOP = 12, 20


def code(value):
    return coded(value, HIDDEN_TOP)


def decode(value):
    return decoded(value, HIDDEN_TOP)


def ring_sum(part, first, begun, gates):
    far = decode(along_z(after(begun, *gates[0]), first)) + part(4 - first)
    close = part(4 + first)
    for left in (2, 1, 0):
        gate = gates[3 - left]
        far = decode(along_z(after(code(far), *gate), first))
        close = decode(along_z(after(code(close), *gate), -first))
        if left:
            far, close = far + part(left * first % Z), close + part(-left * first % Z)
    return far + close + part(0)


def both_yh(value):
    return decode(value) + decode(across_yh(value))


def per_device(tokens, out_grad, w_in, b_in, w_out):
    rows, width = tokens.shape
    units = w_in.shape[1]
    shard = rows * CORES
    row_index = lax.axis_index("row")
    z = row_index // YH

    def place(turn):
        return (z + turn) % Z * shard

    def block(whole, turn):
        return lax.dynamic_slice_in_dim(whole, place(turn), shard, 0)

    tok_panel = spread(joined(tokens))
    grad_pair, tok_panel = lax.optimization_barrier((joined(out_grad), tok_panel))
    grad_panel = spread(grad_pair)

    half_units = units // YH
    yh = row_index % YH
    w_keep = lax.dynamic_slice_in_dim(w_out, yh * half_units, half_units, 0)
    w_send = lax.dynamic_slice_in_dim(w_out, (1 - yh) * half_units, half_units, 0)
    pre_first = code(dot(block(tok_panel, 4), w_in, 1, 0))
    tok_twice = jnp.concatenate([tok_panel, tok_panel], axis=0)
    tok_rolled = lax.dynamic_slice_in_dim(tok_twice, place(0), Z * shard, 0)

    def pre_part(turn):
        return dot(tok_rolled[turn * shard : (turn + 1) * shard], w_in, 1, 0)


    twice = jnp.concatenate([grad_panel, grad_panel], axis=0)
    rolled = lax.dynamic_slice_in_dim(twice, place(6), Z * shard, 0)
    late = 5 * shard
    send_first = code(dot(rolled[late:], w_send, 1, 1))
    came_first = across_yh(send_first)
    send_rest = code(dot(after(rolled, send_first)[:late], w_send, 1, 1))
    came_rest = across_yh(send_rest)

    def back_part(turn):
        slot = (turn + 2) % Z
        keep = dot(rolled[slot * shard : (slot + 1) * shard], w_keep, 1, 1)
        if slot < 5:
            return keep + decode(came_rest[slot * shard : (slot + 1) * shard])
        return keep + decode(came_first[(slot - 5) * shard : (slot - 4) * shard])

    gates = ((), (send_first,), (), ())
    pre = ring_sum(pre_part, 1, pre_first, gates)
    back = ring_sum(back_part, -1, code(back_part(4)), ((), (), (), ()))
    output, slope = gelu_pair(both_yh(code(pre)) + b_in)
    activation = output.astype(jnp.bfloat16)

    def of_half(which, first, second):
        return jnp.where(which == 0, first, second)

    hidden = back * of_half(yh, slope[:, :half_units], slope[:, half_units:])
    hidden = hidden.astype(jnp.bfloat16)

    def ring_gather(value, first):
        got = {0: value}
        up, down = value, value
        for step in (1, 2, 3):
            up, down = along_z(up, 1), along_z(down, -1)
            got[-step % Z], got[step] = up, down
        got[4] = along_z(up if first == 1 else down, first)
        return got

    def laid(got):
        whole = jnp.zeros((Z * shard, units), jnp.bfloat16)
        for turn in (0, 7, 1, 6, 2, 5, 3, 4):
            whole = lax.dynamic_update_slice_in_dim(whole, got[turn], place(turn), 0)
        return whole

    hid_half = ring_gather(hidden, -1)
    act = ring_gather(activation, 1)
    hid = {}
    for group in ((0, 7, 1), (6, 2), (5, 3), (4,)):
        keep = jnp.concatenate([hid_half[turn] for turn in group], axis=0)
        came = across_yh(keep)
        for slot, turn in enumerate(group):
            own = keep[slot * shard : (slot + 1) * shard]
            other = came[slot * shard : (slot + 1) * shard]
            hid[turn] = jnp.concatenate(
                [of_half(yh, own, other), of_half(yh, other, own)], axis=1
            )
    hid_all = laid(hid)

    half = Z * shard // CORES
    theirs = across_core(coded(dot(hid_all[half:], w_in, 1, 1), TOKEN_TOP))
    mine = dot(hid_all[:half], w_in, 1, 1) + decoded(theirs, TOKEN_TOP)
    gw_in = dot(tok_panel, hid_all, 0, 0).astype(jnp.bfloat16)
    sent = once(coded(mine, TOKEN_TOP), gw_in)
    total = mine[:shard]
    for d in range(1, X):
        came = along_x(sent[d * shard : (d + 1) * shard], d)
        total = total + decoded(came, TOKEN_TOP)
    last = coded(total[rows:], TOKEN_TOP)
    grad_tokens = total[:rows] + decoded(across_yl(last), TOKEN_TOP)
    grad_tokens = grad_tokens.astype(jnp.bfloat16)

    act[4] = after(act[4], last)
    act_all = laid(act)
    gw_out = dot(act_all, grad_panel, 0, 0).astype(jnp.bfloat16)
    share = units // (Z * YH)
    own_units = lax.dynamic_slice_in_dim(hid_all, row_index * share, share, 1)
    bias = jnp.sum(own_units.astype(jnp.float32), axis=0)
    return grad_tokens, gw_in, bias, gw_out


def solution(mesh):
    in_specs = (P("col", "row"), P("col", "row"), P("row", "col"), P("col"), P("col", "row"))
    out_specs = (P("col", "row"), P("row", "col"), P(("col", "row")), P("col", "row"))
    return jax.shard_map(
        per_device, mesh=mesh, in_specs=in_specs, out_specs=out_specs, check_vma=False
    )
```

```python
import jax
import jax.numpy as jnp
from jax import lax
from jax.sharding import PartitionSpec as P

gelu_scale = 0.7978845608
cubic = 0.044715
Z, YH, YL, X, CORES = 8, 2, 2, 4, 2
CHIPS = YL * X


def gelu_pair(value):
    inner = jnp.tanh(gelu_scale * (value + cubic * value * value * value))
    output = 0.5 * value * (1.0 + inner)
    slope = 0.5 * (1.0 + inner) + 0.5 * value * (1.0 - inner * inner) * gelu_scale * (
        1.0 + 3.0 * cubic * value * value
    )
    return (output, slope)


def dot(left, right, left_dim, right_dim):
    return lax.dot_general(
        left, right, (((left_dim,), (right_dim,)), ((), ())), preferred_element_type=jnp.float32
    )


def number(z, yh, yl, x, core):
    return (z * YH + yh) * (CHIPS * CORES) + (yl * X + x) * CORES + core


def places():
    for z in range(Z):
        for yh in range(YH):
            for yl in range(YL):
                for x in range(X):
                    for core in range(CORES):
                        yield z, yh, yl, x, core


def permute(value, target):
    pairs = [(number(*place), number(*target(*place))) for place in places()]
    return lax.ppermute(value, ("row", "col"), pairs)


def along_z(value, step):
    return permute(value, lambda z, yh, yl, x, core: ((z + step) % Z, yh, yl, x, core))


def along_x(value, step):
    return permute(value, lambda z, yh, yl, x, core: (z, yh, yl, (x + step) % X, core))


def across_yh(value):
    return permute(value, lambda z, yh, yl, x, core: (z, 1 - yh, yl, x, core))


def across_yl(value):
    return permute(value, lambda z, yh, yl, x, core: (z, yh, 1 - yl, x, core))


def across_core(value):
    return permute(value, lambda z, yh, yl, x, core: (z, yh, yl, x, 1 - core))


def joined(value):
    return jnp.concatenate([value, across_yl(value)], axis=0)


def spread(pair):
    mine = jnp.concatenate([pair] + [along_x(pair, -d) for d in range(1, X)], axis=0)
    return jnp.concatenate([mine, across_core(mine)], axis=0)


def coded(value, top):
    root = jnp.sqrt(jnp.sqrt(jnp.abs(value) * 2.0 ** (60 - top)))
    return jnp.where(value < 0, -root, root).astype(jnp.float16)


def decoded(code, top):
    root = code.astype(jnp.float32)
    return root * jnp.abs(root) * (root * root) * 2.0 ** (top - 60)


def after(value, *others):
    return lax.optimization_barrier((value,) + others)[0]


def once(value, other):
    edge = other[:1, : value.shape[1]]
    return jnp.where(edge != edge, jnp.zeros_like(value), value)


HIDDEN_TOP, TOKEN_TOP = 12, 20


def code(value):
    return coded(value, HIDDEN_TOP)


def decode(value):
    return decoded(value, HIDDEN_TOP)


def ring_sum(part, first, begun, gates):
    far = decode(along_z(after(begun, *gates[0]), first)) + part(4 - first)
    close = part(4 + first)
    for left in (2, 1, 0):
        gate = gates[3 - left]
        far = decode(along_z(after(code(far), *gate), first))
        close = decode(along_z(after(code(close), *gate), -first))
        if left:
            far, close = far + part(left * first % Z), close + part(-left * first % Z)
    return far + close + part(0)


def both_yh(value):
    return decode(value) + decode(across_yh(value))


def per_device(tokens, out_grad, w_in, b_in, w_out):
    rows, width = tokens.shape
    units = w_in.shape[1]
    shard = rows * CORES
    row_index = lax.axis_index("row")
    z = row_index // YH

    def place(turn):
        return (z + turn) % Z * shard

    def block(whole, turn):
        return lax.dynamic_slice_in_dim(whole, place(turn), shard, 0)

    tok_panel = spread(joined(tokens))
    grad_pair, tok_panel = lax.optimization_barrier((joined(out_grad), tok_panel))
    grad_panel = spread(grad_pair)

    half_units = units // YH
    yh = row_index % YH
    w_keep = lax.dynamic_slice_in_dim(w_out, yh * half_units, half_units, 0)
    w_send = lax.dynamic_slice_in_dim(w_out, (1 - yh) * half_units, half_units, 0)
    tok_twice = jnp.concatenate([tok_panel, tok_panel], axis=0)
    tok_rolled = lax.dynamic_slice_in_dim(tok_twice, place(0), Z * shard, 0)
    pre_first = code(dot(tok_rolled[4 * shard : 5 * shard], w_in, 1, 0))

    def pre_part(turn):
        return dot(tok_rolled[turn * shard : (turn + 1) * shard], w_in, 1, 0)


    twice = jnp.concatenate([grad_panel, grad_panel], axis=0)
    rolled = lax.dynamic_slice_in_dim(twice, place(6), Z * shard, 0)
    late = 5 * shard
    send_first = code(dot(rolled[late:], w_send, 1, 1))
    came_first = across_yh(send_first)
    send_rest = code(dot(after(rolled, send_first)[:late], w_send, 1, 1))
    came_rest = across_yh(send_rest)

    def back_part(turn):
        slot = (turn + 2) % Z
        keep = dot(rolled[slot * shard : (slot + 1) * shard], w_keep, 1, 1)
        if slot < 5:
            return keep + decode(came_rest[slot * shard : (slot + 1) * shard])
        return keep + decode(came_first[(slot - 5) * shard : (slot - 4) * shard])

    gates = ((), (send_first,), (), ())
    pre = ring_sum(pre_part, -1, pre_first, gates)
    back = ring_sum(back_part, 1, code(back_part(4)), ((), (), (), ()))
    output, slope = gelu_pair(both_yh(code(pre)) + b_in)
    activation = output.astype(jnp.bfloat16)

    def of_half(which, first, second):
        return jnp.where(which == 0, first, second)

    hidden = back * of_half(yh, slope[:, :half_units], slope[:, half_units:])
    hidden = hidden.astype(jnp.bfloat16)

    def ring_gather(value, first):
        got = {0: value}
        up, down = value, value
        for step in (1, 2, 3):
            up, down = along_z(up, 1), along_z(down, -1)
            got[-step % Z], got[step] = up, down
        got[4] = along_z(up if first == 1 else down, first)
        return got

    def laid(got):
        whole = jnp.zeros((Z * shard, units), jnp.bfloat16)
        for turn in (0, 7, 1, 6, 2, 5, 3, 4):
            whole = lax.dynamic_update_slice_in_dim(whole, got[turn], place(turn), 0)
        return whole

    hid_half = ring_gather(hidden, -1)
    act = ring_gather(activation, 1)
    hid = {}
    for group in ((0, 7, 1), (6, 2), (5, 3), (4,)):
        keep = jnp.concatenate([hid_half[turn] for turn in group], axis=0)
        came = across_yh(keep)
        for slot, turn in enumerate(group):
            own = keep[slot * shard : (slot + 1) * shard]
            other = came[slot * shard : (slot + 1) * shard]
            hid[turn] = jnp.concatenate(
                [of_half(yh, own, other), of_half(yh, other, own)], axis=1
            )
    hid_all = laid(hid)

    half = Z * shard // CORES
    theirs = across_core(coded(dot(hid_all[half:], w_in, 1, 1), TOKEN_TOP))
    mine = dot(hid_all[:half], w_in, 1, 1) + decoded(theirs, TOKEN_TOP)
    gw_in = dot(tok_panel, hid_all, 0, 0).astype(jnp.bfloat16)
    sent = once(coded(mine, TOKEN_TOP), gw_in)
    total = mine[:shard]
    for d in range(1, X):
        came = along_x(sent[d * shard : (d + 1) * shard], d)
        total = total + decoded(came, TOKEN_TOP)
    last = coded(total[rows:], TOKEN_TOP)
    grad_tokens = total[:rows] + decoded(across_yl(last), TOKEN_TOP)
    grad_tokens = grad_tokens.astype(jnp.bfloat16)

    act[4] = after(act[4], last)
    act_all = laid(act)
    gw_out = dot(act_all, grad_panel, 0, 0).astype(jnp.bfloat16)
    share = units // (Z * YH)
    own_units = lax.dynamic_slice_in_dim(hid_all, row_index * share, share, 1)
    bias = jnp.sum(own_units.astype(jnp.float32), axis=0)
    return grad_tokens, gw_in, bias, gw_out


def solution(mesh):
    in_specs = (P("col", "row"), P("col", "row"), P("row", "col"), P("col"), P("col", "row"))
    out_specs = (P("col", "row"), P("row", "col"), P(("col", "row")), P("col", "row"))
    return jax.shard_map(
        per_device, mesh=mesh, in_specs=in_specs, out_specs=out_specs, check_vma=False
    )
```

```python
import jax
import jax.numpy as jnp
from jax import lax
from jax.sharding import PartitionSpec as P

gelu_scale = 0.7978845608
cubic = 0.044715
Z, YH, YL, X, CORES = 8, 2, 2, 4, 2
CHIPS = YL * X


def gelu_pair(value):
    inner = jnp.tanh(gelu_scale * (value + cubic * value * value * value))
    output = 0.5 * value * (1.0 + inner)
    slope = 0.5 * (1.0 + inner) + 0.5 * value * (1.0 - inner * inner) * gelu_scale * (
        1.0 + 3.0 * cubic * value * value
    )
    return (output, slope)


def dot(left, right, left_dim, right_dim):
    return lax.dot_general(
        left, right, (((left_dim,), (right_dim,)), ((), ())), preferred_element_type=jnp.float32
    )


def number(z, yh, yl, x, core):
    return (z * YH + yh) * (CHIPS * CORES) + (yl * X + x) * CORES + core


def places():
    for z in range(Z):
        for yh in range(YH):
            for yl in range(YL):
                for x in range(X):
                    for core in range(CORES):
                        yield z, yh, yl, x, core


def permute(value, target):
    pairs = [(number(*place), number(*target(*place))) for place in places()]
    return lax.ppermute(value, ("row", "col"), pairs)


def along_z(value, step):
    return permute(value, lambda z, yh, yl, x, core: ((z + step) % Z, yh, yl, x, core))


def along_x(value, step):
    return permute(value, lambda z, yh, yl, x, core: (z, yh, yl, (x + step) % X, core))


def across_yh(value):
    return permute(value, lambda z, yh, yl, x, core: (z, 1 - yh, yl, x, core))


def across_yl(value):
    return permute(value, lambda z, yh, yl, x, core: (z, yh, 1 - yl, x, core))


def across_core(value):
    return permute(value, lambda z, yh, yl, x, core: (z, yh, yl, x, 1 - core))


def joined(value):
    return jnp.concatenate([value, across_yl(value)], axis=0)


def spread(pair):
    mine = jnp.concatenate([pair] + [along_x(pair, -d) for d in range(1, X)], axis=0)
    return jnp.concatenate([mine, across_core(mine)], axis=0)


def coded(value, top):
    root = jnp.sqrt(jnp.sqrt(jnp.abs(value) * 2.0 ** (60 - top)))
    return jnp.where(value < 0, -root, root).astype(jnp.float16)


def decoded(code, top):
    root = code.astype(jnp.float32)
    return root * jnp.abs(root) * (root * root) * 2.0 ** (top - 60)


def after(value, *others):
    return lax.optimization_barrier((value,) + others)[0]


def once(value, other):
    edge = other[:1, : value.shape[1]]
    return jnp.where(edge != edge, jnp.zeros_like(value), value)


HIDDEN_TOP, TOKEN_TOP = 12, 20


def code(value):
    return coded(value, HIDDEN_TOP)


def decode(value):
    return decoded(value, HIDDEN_TOP)


def ring_sum(part, first, begun, gates):
    far = decode(along_z(after(begun, *gates[0]), first)) + part(4 - first)
    close = part(4 + first)
    for left in (2, 1, 0):
        gate = gates[3 - left]
        far = decode(along_z(after(code(far), *gate), first))
        close = decode(along_z(after(code(close), *gate), -first))
        if left:
            far, close = far + part(left * first % Z), close + part(-left * first % Z)
    return far + close + part(0)


def both_yh(value):
    return decode(value) + decode(across_yh(value))


def per_device(tokens, out_grad, w_in, b_in, w_out):
    rows, width = tokens.shape
    units = w_in.shape[1]
    shard = rows * CORES
    row_index = lax.axis_index("row")
    z = row_index // YH

    def place(turn):
        return (z + turn) % Z * shard

    def block(whole, turn):
        return lax.dynamic_slice_in_dim(whole, place(turn), shard, 0)

    tok_panel = spread(joined(tokens))
    grad_pair, tok_panel = lax.optimization_barrier((joined(out_grad), tok_panel))
    grad_panel = spread(grad_pair)

    half_units = units // YH
    yh = row_index % YH
    w_keep = lax.dynamic_slice_in_dim(w_out, yh * half_units, half_units, 0)
    w_send = lax.dynamic_slice_in_dim(w_out, (1 - yh) * half_units, half_units, 0)
    tok_twice = jnp.concatenate([tok_panel, tok_panel], axis=0)
    tok_rolled = lax.dynamic_slice_in_dim(tok_twice, place(0), Z * shard, 0)
    pre_first = code(dot(tok_rolled[4 * shard : 5 * shard], w_in, 1, 0))

    def pre_part(turn):
        return dot(tok_rolled[turn * shard : (turn + 1) * shard], w_in, 1, 0)


    twice = jnp.concatenate([grad_panel, grad_panel], axis=0)
    rolled = lax.dynamic_slice_in_dim(twice, place(6), Z * shard, 0)
    late = 5 * shard
    send_first = code(dot(rolled[late:], w_send, 1, 1))
    came_first = across_yh(send_first)
    send_rest = code(dot(after(rolled, send_first)[:late], w_send, 1, 1))
    came_rest = across_yh(send_rest)

    def back_part(turn):
        slot = (turn + 2) % Z
        keep = dot(rolled[slot * shard : (slot + 1) * shard], w_keep, 1, 1)
        if slot < 5:
            return keep + decode(came_rest[slot * shard : (slot + 1) * shard])
        return keep + decode(came_first[(slot - 5) * shard : (slot - 4) * shard])

    gates = ((), (send_first,), (), ())
    pre = ring_sum(pre_part, -1, pre_first, gates)
    back = ring_sum(back_part, 1, code(back_part(4)), ((), (), (), ()))
    output, slope = gelu_pair(both_yh(code(pre)) + b_in)
    activation = output.astype(jnp.bfloat16)

    def of_half(which, first, second):
        return jnp.where(which == 0, first, second)

    hidden = back * of_half(yh, slope[:, :half_units], slope[:, half_units:])
    hidden = hidden.astype(jnp.bfloat16)

    def ring_gather(value, first):
        got = {0: value}
        up, down = value, value
        for step in (1, 2, 3):
            up, down = along_z(up, 1), along_z(down, -1)
            got[-step % Z], got[step] = up, down
        got[4] = along_z(up if first == 1 else down, first)
        return got

    def laid(got):
        whole = jnp.zeros((Z * shard, units), jnp.bfloat16)
        for turn in (0, 7, 1, 6, 2, 5, 3, 4):
            whole = lax.dynamic_update_slice_in_dim(whole, got[turn], place(turn), 0)
        return whole

    hid_half = ring_gather(hidden, -1)
    act = ring_gather(activation, 1)
    hid = {}
    for group in ((0, 7, 1), (6, 2), (5, 3), (4,)):
        keep = jnp.concatenate([hid_half[turn] for turn in group], axis=0)
        came = across_yh(keep)
        for slot, turn in enumerate(group):
            own = keep[slot * shard : (slot + 1) * shard]
            other = came[slot * shard : (slot + 1) * shard]
            hid[turn] = jnp.concatenate(
                [of_half(yh, own, other), of_half(yh, other, own)], axis=1
            )
    hid_all = laid(hid)

    half = Z * shard // CORES
    theirs = across_core(coded(dot(hid_all[half:], w_in, 1, 1), TOKEN_TOP))
    mine = dot(hid_all[:half], w_in, 1, 1) + decoded(theirs, TOKEN_TOP)
    gw_in = dot(tok_panel, hid_all, 0, 0).astype(jnp.bfloat16)
    sent = once(coded(mine, TOKEN_TOP), gw_in)
    total = mine[:shard]
    for d in range(1, X):
        came = along_x(sent[d * shard : (d + 1) * shard], d)
        total = total + decoded(came, TOKEN_TOP)
    last = coded(total[rows:], TOKEN_TOP)
    grad_tokens = total[:rows] + decoded(across_yl(last), TOKEN_TOP)
    grad_tokens = grad_tokens.astype(jnp.bfloat16)

    act[4] = after(act[4], last)
    act_all = laid(act)
    gw_out = dot(act_all, grad_panel, 0, 0).astype(jnp.bfloat16)
    share = units // (Z * YH)
    own_units = lax.dynamic_slice_in_dim(hid_all, row_index * share, share, 1)
    bias = jnp.sum(once(own_units, sent).astype(jnp.float32), axis=0)
    return grad_tokens, gw_in, bias, gw_out


def solution(mesh):
    in_specs = (P("col", "row"), P("col", "row"), P("row", "col"), P("col"), P("col", "row"))
    out_specs = (P("col", "row"), P("row", "col"), P(("col", "row")), P("col", "row"))
    return jax.shard_map(
        per_device, mesh=mesh, in_specs=in_specs, out_specs=out_specs, check_vma=False
    )
```
